128 devices in a mesh: row: 8 (over z, y_lo), col: 16 (over y_hi, x, core).
Axes of the slice: x: 4, y: 4 (y_hi: 2, y_lo: 2; y = y_hi * 2 + y_lo), z: 4, core: 2. Of those that a mesh axis runs over, the one named last changes fastest.
Arguments:
- integrals: float32 [3072, 16384], P('row', 'col'), may hold values from -0.046875 to 0.046875
- amplitudes: float32 [32, 512, 8, 512], P('row', 'col'), may hold values from -6 to 6
- driver: float32 [3072, 4096], P('row', 'col'), may hold values from -6 to 6
- occ_rows: float32 [6], replicated, may hold values from -2 to -0.5
- occ_cols: float32 [8], replicated, may hold values from -2 to -0.5
- virtual: float32 [512], replicated, may hold values from 0.2 to 3
Outputs:
- updated: float32 [3072, 4096], P('row', 'col')
The draws below stay inside these ranges and needn't reach their ends.
All inputs are finite; a program needn't handle non-finite values.
Results may differ from the reference program's by a relative error of at most 0.000062.
Values sent between devices are 32-bit elements; how exact they have to be, the bound alone decides.
No kernel may reach another device: no remote copies, remote signals or barrier semaphores. Data moves between devices by JAX's collectives and lax.ppermute only.
A program may use at most 128 MiB of HBM per device.

```python
import jax
import jax.numpy as jnp
from jax import lax

V = 512
KO = 32
OI = 6
OJ = 8
KC = 16384
ROWS = 3072
COLS = 4096


def levels(stream_key, extent, shards, low, top_value):
    def one(dim, shards_of):
        draws = jax.random.uniform(jax.random.fold_in(jax.random.fold_in(stream_key, 6), dim), (shards_of,), jnp.float32, low / len(shards), top_value / len(shards))
        return jnp.repeat(jnp.exp(draws), extent[dim] // shards_of).reshape((-1,) + (1,) * (len(extent) - dim - 1))

    loudness = one(*shards[0])
    for cut in shards[1:]:
        loudness = loudness * one(*cut)
    return loudness


def normal_values(stream_key, dims, spread, most, split=(), dtype=jnp.bfloat16):
    drawn = jax.random.normal(stream_key, dims, jnp.float32) * spread
    if len(split) > 0:
        drawn = levels(stream_key, dims, split, -0.22, 0.18) * drawn
    return jnp.clip(drawn, min=-most, max=most).astype(dtype)


def setup_inputs(seed: int = 0) -> dict:
    seeds = jax.random.split(jax.random.key(seed), 7)
    return {
        "integrals": normal_values(seeds[0], (ROWS, KC), KC ** -0.5, 0.046875, ((0, 8), (1, 16)), jnp.float32),
        "amplitudes": normal_values(seeds[1], (KO, V, OJ, V), 1.0, 6.0, ((0, 8), (1, 16)), jnp.float32),
        "driver": normal_values(seeds[2], (ROWS, COLS), 1.0, 6.0, ((0, 8), (1, 16)), jnp.float32),
        "occ_rows": jnp.clip(jax.random.uniform(seeds[3], (OI,), jnp.float32, -2.0, -0.5), -2.0, -0.5),
        "occ_cols": jnp.clip(jax.random.uniform(seeds[4], (OJ,), jnp.float32, -2.0, -0.5), -2.0, -0.5),
        "virtual": jnp.clip(jax.random.uniform(seeds[5], (V,), jnp.float32, 0.2, 3.0), 0.2, 3.0),
    }


def reference(integrals, amplitudes, driver, occ_rows, occ_cols, virtual):
    amp_matrix = amplitudes.reshape(KO * V, OJ * V)
    cycle = jnp.dot(integrals, amp_matrix, precision=lax.Precision.HIGHEST, preferred_element_type=jnp.float32)
    row_energy = (occ_rows[:, None] - virtual[None, :]).reshape(OI * V)
    col_energy = (occ_cols[:, None] - virtual[None, :]).reshape(OJ * V)
    denominator = row_energy[:, None] + col_energy[None, :]
    return (driver + cycle) / denominator
```

```python
import jax
import jax.numpy as jnp
from jax import lax
from jax.sharding import Mesh, PartitionSpec as P

AXES = ("z", "yl", "yh", "x", "core")
SIZES = (4, 2, 2, 4, 2)


def device_index(z, y, x, core):
    return (((z * 2 + y % 2) * 2 + y // 2) * 4 + x) * 2 + core


def moves(target):
    pairs = []
    for z in range(4):
        for y in range(4):
            for x in range(4):
                for core in range(2):
                    pairs.append((device_index(z, y, x, core), device_index(*target(z, y, x, core))))
    return pairs


RING_Z = moves(lambda z, y, x, core: ((z + 1 - 2 * core) % 4, y, x, core))
RING_Y = moves(lambda z, y, x, core: (z, (y + 1 - 2 * core) % 4, x, core))
SWAP = moves(lambda z, y, x, core: (z, y, x, 1 - core))


def ring(own, pairs):
    held = [own]
    for _ in range(3):
        held.append(lax.ppermute(held[-1], AXES, pairs))
    return held


def in_order(held, position, core):
    step = 1 - 2 * core
    stacked = jnp.stack(held)
    return jnp.take(stacked, (step * (position - jnp.arange(4))) % 4, axis=0)


def shards(integrals, amplitudes, driver, occ_rows, occ_cols, virtual):
    z, yl, yh, x, core = (lax.axis_index(axis) for axis in AXES)
    y = yh * 2 + yl
    rows = driver.shape[0]
    amp = amplitudes.reshape(4, 32, 2, 4, 2, 2, 128).transpose(2, 5, 4, 0, 1, 3, 6).reshape(4, 2, 128, 512)
    amp = lax.all_to_all(amp, ("yh", "yl"), 0, 0, tiled=True)
    ints = integrals.reshape(rows, 2, 2, 4, 2, 32).transpose(3, 4, 0, 1, 2, 5).reshape(8, rows, 128)
    ints = lax.all_to_all(ints, ("x", "core"), 0, 0, tiled=True)
    amp = in_order(ring(amp, RING_Z), z, core)
    ints = in_order(ring(ints, RING_Y), y, core)
    lhs = ints.reshape(2, 2, 8, rows, 128).transpose(1, 3, 0, 2, 4).reshape(2 * rows, 2048)
    rhs = amp.reshape(4, 2, 2, 2, 4, 32, 512).transpose(0, 2, 4, 1, 5, 3, 6).reshape(2048, 1024)
    part = jnp.dot(lhs, rhs, precision=lax.Precision.HIGH, preferred_element_type=jnp.float32)
    part = part.reshape(2, rows, 2, 4, 128)
    other = lax.dynamic_index_in_dim(part, 1 - core, 2, keepdims=False)
    mine = lax.dynamic_index_in_dim(part, core, 2, keepdims=False)
    mine = mine + lax.ppermute(other, AXES, SWAP)
    mine = mine.transpose(0, 2, 1, 3).reshape(8, rows, 128)
    mine = lax.all_to_all(mine, ("yl", "x"), 0, 0, tiled=True)
    cycle = mine.reshape(2, 4, rows, 128).sum(axis=1).transpose(1, 0, 2).reshape(rows, 256)
    row_energy = (occ_rows[:, None] - virtual[None, :]).reshape(-1)
    col_energy = (occ_cols[:, None] - virtual[None, :]).reshape(-1)
    row_part = lax.dynamic_slice_in_dim(row_energy, (z * 2 + yl) * rows, rows, 0)
    col_part = lax.dynamic_slice_in_dim(col_energy, ((yh * 4 + x) * 2 + core) * 256, 256, 0)
    denominator = row_part[:, None] + col_part[None, :]
    return (driver + cycle) / denominator


def solution(mesh):
    fine = Mesh(mesh.devices.reshape(SIZES), AXES)
    row, col = ("z", "yl"), ("yh", "x", "core")
    in_specs = (P(row, col), P(row, col, None, None), P(row, col), P(), P(), P())
    return jax.shard_map(shards, mesh=fine, in_specs=in_specs, out_specs=P(row, col), check_vma=False)
```

```python
import functools

import jax
import jax.numpy as jnp
from jax import lax
from jax.experimental import pallas as pl
from jax.experimental.pallas import tpu as pltpu
from jax.sharding import Mesh, PartitionSpec as P

AXES = ("z", "yl", "yh", "x", "core")
SIZES = (4, 2, 2, 4, 2)
F32, BF16 = jnp.float32, jnp.bfloat16


def device_index(z, y, x, core):
    return (((z * 2 + y % 2) * 2 + y // 2) * 4 + x) * 2 + core


def moves(target):
    pairs = []
    for z in range(4):
        for y in range(4):
            for x in range(4):
                for core in range(2):
                    pairs.append((device_index(z, y, x, core), device_index(*target(z, y, x, core))))
    return pairs


Z_ON = [moves(lambda z, y, x, core, d=d: ((z + d * (1 - 2 * core)) % 4, y, x, core)) for d in range(4)]
Y_ON = [moves(lambda z, y, x, core, d=d: (z, (y + d * (1 - 2 * core)) % 4, x, core)) for d in range(4)]
SWAP = moves(lambda z, y, x, core: (z, y, x, 1 - core))


def call(body, grid, in_specs, out_specs, out_shape, scalars, operands, scratch=(), aliases=None, flops=0, vmem=8 << 20):
    nbytes = sum(4 * o.size for o in operands[:1])
    return pl.pallas_call(
        body,
        grid_spec=pltpu.PrefetchScalarGridSpec(
            num_scalar_prefetch=1, grid=grid, in_specs=in_specs, out_specs=out_specs, scratch_shapes=list(scratch)
        ),
        out_shape=out_shape,
        input_output_aliases=aliases or {},
        cost_estimate=pl.CostEstimate(flops=flops, bytes_accessed=2 * nbytes, transcendentals=0),
        compiler_params=pltpu.CompilerParams(vmem_limit_bytes=vmem),
    )(scalars, *operands)


def split_amplitudes(amplitudes, targets):
    def body(target, src, *refs):
        outs, turned = refs[:4], refs[4]
        turned[...] = jnp.swapaxes(src[0], 0, 1)
        for out, slot in zip(outs, range(4)):
            y = target[slot]
            yh, yl = y // 2, y % 2
            for half in range(2):
                lanes = pl.ds(pl.multiple_of(half * 256 + yl * 128, 128), 128)
                for x in range(4):
                    out[half, :, x * 128 : (x + 1) * 128] = turned[yh * 4 + x, :, lanes]

    return call(
        body,
        (4,),
        [pl.BlockSpec((1, 32, 8, 512), lambda k, t: (k, 0, 0, 0))],
        [pl.BlockSpec((2, 32, 512), lambda k, t: (0, k, 0))] * 4,
        [jax.ShapeDtypeStruct((2, 128, 512), F32)] * 4,
        targets,
        (amplitudes,),
        scratch=[pltpu.VMEM((8, 32, 512), F32)],
    )


def split_integrals(integrals):
    rows = integrals.shape[0]
    step = rows // 3

    def body(unused, src, out):
        lane = lax.broadcasted_iota(jnp.int32, (step, 128), 1) // 32
        for h in range(2):
            tiles = [src[:, (e * 4 + yh * 2 + h) * 128 :][:, :128] for yh in range(2) for e in range(2)]
            for j in range(4):
                made = None
                for s in range(4):
                    turn = (s - j) % 4 * 32
                    moved = pltpu.roll(tiles[s], turn, 1) if turn else tiles[s]
                    made = moved if made is None else jnp.where(lane == s, moved, made)
                out[h * 4 + j] = made

    return call(
        body,
        (3,),
        [pl.BlockSpec((step, 1024), lambda r, t: (r, 0))],
        pl.BlockSpec((8, step, 128), lambda r, t: (0, r, 0)),
        jax.ShapeDtypeStruct((8, rows, 128), F32),
        jnp.zeros((1,), jnp.int32),
        (integrals,),
    )


def two_parts(value):
    high = value.astype(BF16)
    return high, (value - high.astype(F32)).astype(BF16)


def laid_out(src, rows):
    first = lax.broadcasted_iota(jnp.int32, (rows, 128), 1) < 64
    for z0 in range(src.shape[0] // 4):
        for yb in range(2):
            one, two = src[z0 * 4 + yb * 2], src[z0 * 4 + yb * 2 + 1]
            yield (z0 * 2 + 0) * 2 + yb, jnp.where(first, one, pltpu.roll(two, 64, 1))
            yield (z0 * 2 + 1) * 2 + yb, jnp.where(first, pltpu.roll(one, 64, 1), two)


def product(ah, al, bh, bl):
    dot = functools.partial(jnp.dot, preferred_element_type=F32)
    return dot(ah, bh) + (dot(ah, bl) + dot(al, bh))


ANY = pl.BlockSpec(memory_space=pl.ANY)
VMEM_FIRST, VMEM_LAST = 56 << 20, 20 << 20
SMALL = pl.BlockSpec(memory_space=pltpu.SMEM)


def first_products(place, ints, own, near):
    rows = ints[0].shape[1]

    def body(at, *refs):
        src_a, src_own, src_near = refs[:3], refs[3:7], refs[7:10]
        out_a, out_b, sums = refs[10:12], refs[12:14], refs[14:16]
        raw_a, raw_own, raw_near, a, b, total, sem, done = refs[16:]
        core, z, y = at[0], at[1], at[2]
        way = 1 - 2 * core
        yl, yh = y & 1, y // 2
        zh, z0 = ((z + 2) & 3) // 2, z & 1
        halves = (1 - core, core)
        loads_a = [pltpu.make_async_copy(src_a[n], raw_a.at[n], sem.at[n]) for n in range(3)]
        loads_b = []
        for n, half in enumerate(halves):
            loads_b.append(
                [pltpu.make_async_copy(src_own[s].at[half], raw_own.at[n, s], sem.at[3 + n * 7 + s]) for s in range(4)]
                + [pltpu.make_async_copy(src_near[s].at[half], raw_near.at[n, s], sem.at[7 + n * 7 + s]) for s in range(3)]
            )
        for copy in loads_a + loads_b[0] + loads_b[1]:
            copy.start()
        stores = []

        def store(source, target):
            stores.append(pltpu.make_async_copy(source, target, done.at[len(stores)]))
            stores[-1].start()

        steps = (0, 1, 3)
        for n, step in enumerate(steps):
            loads_a[n].wait()
            slot = (y - step * way) & 3
            for tile, value in laid_out(raw_a.at[n], rows):
                lanes = slice(tile % 4 * 128, tile % 4 * 128 + 128)
                a[slot, tile // 4, 0, :, lanes], a[slot, tile // 4, 1, :, lanes] = two_parts(value)
        store(a.at[y, z0], out_a[0])
        store(a.at[zh * 2 + 1 - yl, z0], out_a[1])
        for n, half in enumerate(halves):
            for copy in loads_b[n]:
                copy.wait()
            for s in range(4):
                slot = (z - s * way) & 3
                b[n, slot, 0, y], b[n, slot, 1, y] = two_parts(raw_own[n, s])
            for m, back in enumerate((1, 3, 2)):
                part = (y - back * way) & 3
                for k, step in enumerate(steps):
                    slot = (z - step * way) & 3
                    b[n, slot, 0, part], b[n, slot, 1, part] = two_parts(raw_near[n, k, m])
                empty = jnp.zeros((128, 512), BF16)
                b[n, (z + 2) & 3, 0, part], b[n, (z + 2) & 3, 1, part] = empty, empty
            store(b.at[n, pl.ds((1 - yh) * 2, 2)], out_b[n])
            for group, chosen in ((yl, (0,)), (1 - yl, (1, 3))):
                value = None
                for step in chosen:
                    slot = (y - step * way) & 3
                    for k in range(2):
                        bh, bl = (b[n, slot // 2 * 2 + k, p].reshape(512, 512) for p in range(2))
                        part = product(a[slot, k, 0], a[slot, k, 1], bh, bl)
                        value = part if value is None else value + part
                total[n, group] = value
            store(total.at[n], sums[n])
        for copy in stores:
            copy.wait()

    return pl.pallas_call(
        body,
        in_specs=[SMALL] + [ANY] * 10,
        out_specs=[ANY] * 6,
        out_shape=[jax.ShapeDtypeStruct((2, rows, 512), BF16)] * 2
        + [jax.ShapeDtypeStruct((2, 2, 4, 128, 512), BF16)] * 2
        + [jax.ShapeDtypeStruct((2, rows, 512), F32)] * 2,
        scratch_shapes=[
            pltpu.VMEM((3, 8, rows, 128), F32),
            pltpu.VMEM((2, 4, 128, 512), F32),
            pltpu.VMEM((2, 3, 3, 128, 512), F32),
            pltpu.VMEM((4, 2, 2, rows, 512), BF16),
            pltpu.VMEM((2, 4, 2, 4, 128, 512), BF16),
            pltpu.VMEM((2, 2, rows, 512), F32),
            pltpu.SemaphoreType.DMA((17,)),
            pltpu.SemaphoreType.DMA((6,)),
        ],
        cost_estimate=pl.CostEstimate(flops=18 * rows * 2048 * 512, bytes_accessed=24 << 20, transcendentals=0),
        compiler_params=pltpu.CompilerParams(vmem_limit_bytes=VMEM_FIRST),
    )(place, *ints, *own, *near)


def last_products(place, sums, ints, near, own_a, other_a, far_b):
    rows = sums.shape[1]

    def body(at, src_sum, src_far, src_near, src_own, src_other, src_b, out, *refs):
        total, raw, raw_near, own, other, far, b, late, sem = refs
        half, z, y, core = at[0], at[1], at[2], at[3]
        way = 1 - 2 * core
        yl, yh = y & 1, y // 2
        zh, z0 = ((z + 2) & 3) // 2, z & 1
        pairs = (src_near.at[half], raw_near), (src_far, raw), (src_other, other), (src_sum, total), (src_own, own), (src_b, b)
        copies = [pltpu.make_async_copy(*pair, sem.at[n]) for n, pair in enumerate(pairs)]
        for copy in copies:
            copy.start()
        copies[0].wait()
        empty = jnp.zeros((128, 512), BF16)
        late[0, y], late[1, y] = empty, empty
        for m, back in enumerate((1, 3, 2)):
            slot = (y - back * way) & 3
            late[0, slot], late[1, slot] = two_parts(raw_near[m])
        bh, bl = late[0].reshape(512, 512), late[1].reshape(512, 512)
        copies[1].wait()
        for tile, value in laid_out(raw, rows):
            lanes = slice(tile % 4 * 128, tile % 4 * 128 + 128)
            far[tile // 4, 0, :, lanes], far[tile // 4, 1, :, lanes] = two_parts(value)
        for copy in copies[2:5]:
            copy.wait()
        value = total[1 - yl] + product(other[0], other[1], bh, bl)
        for x in range(4):
            out[(1 - yl) * 4 + x] = value[:, x * 128 : x * 128 + 128]

        @pl.when(yh != zh)
        def _():
            own[...] = far[z0]

        value = total[yl] + product(own[0], own[1], bh, bl)
        copies[5].wait()
        for k in range(2):
            value = value + product(far[k, 0], far[k, 1], *(b[k, p].reshape(512, 512) for p in range(2)))
        for x in range(4):
            out[yl * 4 + x] = value[:, x * 128 : x * 128 + 128]

    return pl.pallas_call(
        body,
        in_specs=[SMALL] + [ANY] * 6,
        out_specs=pl.BlockSpec(memory_space=pltpu.VMEM),
        out_shape=jax.ShapeDtypeStruct((8, rows, 128), F32),
        scratch_shapes=[
            pltpu.VMEM((2, rows, 512), F32),
            pltpu.VMEM((8, rows, 128), F32),
            pltpu.VMEM((3, 128, 512), F32),
            pltpu.VMEM((2, rows, 512), BF16),
            pltpu.VMEM((2, rows, 512), BF16),
            pltpu.VMEM((2, 2, rows, 512), BF16),
            pltpu.VMEM((2, 2, 4, 128, 512), BF16),
            pltpu.VMEM((2, 4, 128, 512), BF16),
            pltpu.SemaphoreType.DMA((6,)),
        ],
        cost_estimate=pl.CostEstimate(flops=6 * rows * 2048 * 512, bytes_accessed=8 << 20, transcendentals=0),
        compiler_params=pltpu.CompilerParams(vmem_limit_bytes=VMEM_LAST),
    )(place, sums, ints, near, own_a, other_a, far_b)


def total_of(one, two):
    def body(a, b, out):
        out[...] = a[...] + b[...]

    whole = pl.BlockSpec(memory_space=pltpu.VMEM)
    return pl.pallas_call(
        body,
        in_specs=[whole] * 2,
        out_specs=whole,
        out_shape=jax.ShapeDtypeStruct(one.shape, F32),
        compiler_params=pltpu.CompilerParams(vmem_limit_bytes=4 << 20),
    )(one, two)


def finish(parts, driver, row_part, col_part):
    rows = driver.shape[0]
    step = rows // 3

    def body(unused, part, given, row, col, out):
        for yl in range(2):
            lanes = slice(yl * 128, (yl + 1) * 128)
            cycle = (part[yl * 4] + part[yl * 4 + 1]) + (part[yl * 4 + 2] + part[yl * 4 + 3])
            out[:, lanes] = (given[:, lanes] + cycle) / (row[...] + col[:, lanes])

    return call(
        body,
        (3,),
        [
            pl.BlockSpec((8, step, 128), lambda r, t: (0, r, 0)),
            pl.BlockSpec((step, 256), lambda r, t: (r, 0)),
            pl.BlockSpec((step, 1), lambda r, t: (r, 0)),
            pl.BlockSpec((1, 256), lambda r, t: (0, 0)),
        ],
        pl.BlockSpec((step, 256), lambda r, t: (r, 0)),
        jax.ShapeDtypeStruct((rows, 256), F32),
        jnp.zeros((1,), jnp.int32),
        (parts, driver, row_part, col_part),
    )


def shards(integrals, amplitudes, driver, occ_rows, occ_cols, virtual):
    z, yl, yh, x, core = (lax.axis_index(axis) for axis in AXES)
    y = yh * 2 + yl
    way = 1 - 2 * core
    rows = driver.shape[0]
    number = lambda *v: jnp.stack([jnp.asarray(i, jnp.int32) for i in v])

    ints = split_integrals(integrals)
    amplitudes, ints = lax.optimization_barrier((amplitudes, ints))
    parts = split_amplitudes(amplitudes, number(*((y + d * way) % 4 for d in range(4))))
    on_z = lambda v, d: lax.ppermute(v, AXES, Z_ON[d])
    on_y = lambda v, d: lax.ppermute(v, AXES, Y_ON[d])
    wave = lambda *v: list(lax.optimization_barrier(v))
    ints = lax.all_to_all(ints, ("x", "core"), 0, 0, tiled=True)
    b, c, d = on_y(parts[1], 1), on_y(parts[3], 3), on_y(parts[2], 2)
    own = [parts[0]] + [on_z(parts[0], step) for step in (1, 2, 3)]
    ints, b, c, d, *own[1:] = wave(ints, b, c, d, *own[1:])
    bcd = jnp.stack([b, c, d], axis=1)
    bcd1, bcd3, ints1, ints3 = wave(on_z(bcd, 1), on_z(bcd, 3), on_y(ints, 1), on_y(ints, 3))
    bcd2, ints2 = on_z(bcd1, 1), on_y(ints1, 1)
    own_a, other_a, far_other, far_mine, sum_other, sum_mine = first_products(
        number(core, z, y), (ints, ints1, ints3), own, (bcd, bcd1, bcd3)
    )
    bcd2, ints2 = wave(bcd2, ints2)
    other = last_products(number(1 - core, z, y, core), sum_other, ints2, bcd2, own_a, other_a, far_other)
    mine = last_products(number(core, z, y, core), sum_mine, ints2, bcd2, own_a, other_a, far_mine)
    mine = total_of(mine, lax.ppermute(other, AXES, SWAP))
    mine = lax.all_to_all(mine, ("yl", "x"), 0, 0, tiled=True)
    row_energy = (occ_rows[:, None] - virtual[None, :]).reshape(-1)
    col_energy = (occ_cols[:, None] - virtual[None, :]).reshape(-1)
    row_part = lax.dynamic_slice_in_dim(row_energy, (z * 2 + yl) * rows, rows, 0)
    col_part = lax.dynamic_slice_in_dim(col_energy, ((yh * 4 + x) * 2 + core) * 256, 256, 0)
    return finish(mine, driver, row_part[:, None], col_part[None, :])


def solution(mesh):
    fine = Mesh(mesh.devices.reshape(SIZES), AXES)
    row, col = ("z", "yl"), ("yh", "x", "core")
    in_specs = (P(row, col), P(row, col, None, None), P(row, col), P(), P(), P())
    return jax.shard_map(shards, mesh=fine, in_specs=in_specs, out_specs=P(row, col), check_vma=False)
```

```python
import functools

import jax
import jax.numpy as jnp
from jax import lax
from jax.experimental import pallas as pl
from jax.experimental.pallas import tpu as pltpu
from jax.sharding import Mesh, PartitionSpec as P

AXES = ("z", "yl", "yh", "x", "core")
SIZES = (4, 2, 2, 4, 2)
F32, BF16 = jnp.float32, jnp.bfloat16


def device_index(z, y, x, core):
    return (((z * 2 + y % 2) * 2 + y // 2) * 4 + x) * 2 + core


def moves(target):
    pairs = []
    for z in range(4):
        for y in range(4):
            for x in range(4):
                for core in range(2):
                    pairs.append((device_index(z, y, x, core), device_index(*target(z, y, x, core))))
    return pairs


Z_ON = [moves(lambda z, y, x, core, d=d: ((z + d * (1 - 2 * core)) % 4, y, x, core)) for d in range(4)]
Y_ON = [moves(lambda z, y, x, core, d=d: (z, (y + d * (1 - 2 * core)) % 4, x, core)) for d in range(4)]
SWAP = moves(lambda z, y, x, core: (z, y, x, 1 - core))


def call(body, grid, in_specs, out_specs, out_shape, scalars, operands, scratch=(), aliases=None, flops=0, vmem=8 << 20):
    nbytes = sum(4 * o.size for o in operands[:1])
    return pl.pallas_call(
        body,
        grid_spec=pltpu.PrefetchScalarGridSpec(
            num_scalar_prefetch=1, grid=grid, in_specs=in_specs, out_specs=out_specs, scratch_shapes=list(scratch)
        ),
        out_shape=out_shape,
        input_output_aliases=aliases or {},
        cost_estimate=pl.CostEstimate(flops=flops, bytes_accessed=2 * nbytes, transcendentals=0),
        compiler_params=pltpu.CompilerParams(vmem_limit_bytes=vmem),
    )(scalars, *operands)


def split_amplitudes(amplitudes, targets):
    def body(target, src, *refs):
        outs, turned = refs[:4], refs[4]
        turned[...] = jnp.swapaxes(src[0], 0, 1)
        for out, slot in zip(outs, range(4)):
            y = target[slot]
            yh, yl = y // 2, y % 2
            for half in range(2):
                lanes = pl.ds(pl.multiple_of(half * 256 + yl * 128, 128), 128)
                for x in range(4):
                    out[half, :, x * 128 : (x + 1) * 128] = turned[yh * 4 + x, :, lanes]

    return call(
        body,
        (4,),
        [pl.BlockSpec((1, 32, 8, 512), lambda k, t: (k, 0, 0, 0))],
        [pl.BlockSpec((2, 32, 512), lambda k, t: (0, k, 0))] * 4,
        [jax.ShapeDtypeStruct((2, 128, 512), F32)] * 4,
        targets,
        (amplitudes,),
        scratch=[pltpu.VMEM((8, 32, 512), F32)],
    )


def split_integrals(integrals):
    rows = integrals.shape[0]
    step = rows // 3

    def body(unused, src, out):
        lane = lax.broadcasted_iota(jnp.int32, (step, 128), 1) // 32
        for h in range(2):
            tiles = [src[:, (e * 4 + yh * 2 + h) * 128 :][:, :128] for yh in range(2) for e in range(2)]
            for j in range(4):
                made = None
                for s in range(4):
                    turn = (s - j) % 4 * 32
                    moved = pltpu.roll(tiles[s], turn, 1) if turn else tiles[s]
                    made = moved if made is None else jnp.where(lane == s, moved, made)
                out[h * 4 + j] = made

    return call(
        body,
        (3,),
        [pl.BlockSpec((step, 1024), lambda r, t: (r, 0))],
        pl.BlockSpec((8, step, 128), lambda r, t: (0, r, 0)),
        jax.ShapeDtypeStruct((8, rows, 128), F32),
        jnp.zeros((1,), jnp.int32),
        (integrals,),
    )


def two_parts(value):
    high = value.astype(BF16)
    return high, (value - high.astype(F32)).astype(BF16)


def laid_out(src, rows):
    first = lax.broadcasted_iota(jnp.int32, (rows, 128), 1) < 64
    for z0 in range(src.shape[0] // 4):
        for yb in range(2):
            one, two = src[z0 * 4 + yb * 2], src[z0 * 4 + yb * 2 + 1]
            yield (z0 * 2 + 0) * 2 + yb, jnp.where(first, one, pltpu.roll(two, 64, 1))
            yield (z0 * 2 + 1) * 2 + yb, jnp.where(first, pltpu.roll(one, 64, 1), two)


def product(ah, al, bh, bl):
    dot = functools.partial(jnp.dot, preferred_element_type=F32)
    return dot(ah, bh) + (dot(ah, bl) + dot(al, bh))


ANY = pl.BlockSpec(memory_space=pl.ANY)
VMEM_FIRST, VMEM_LAST = 56 << 20, 20 << 20
SMALL = pl.BlockSpec(memory_space=pltpu.SMEM)


def first_products(place, ints, own, near):
    rows = ints[0].shape[1]

    def body(at, *refs):
        src_a, src_own, src_near = refs[:3], refs[3:7], refs[7:10]
        out_a, out_b, sums = refs[10:12], refs[12:14], refs[14:16]
        raw_a, raw_own, raw_near, a, b, total, sem, done = refs[17:]
        refs[16][...] = jnp.zeros((8, 128), F32)
        core, z, y = at[0], at[1], at[2]
        way = 1 - 2 * core
        yl, yh = y & 1, y // 2
        zh, z0 = ((z + 2) & 3) // 2, z & 1
        halves = (1 - core, core)
        loads_a = [pltpu.make_async_copy(src_a[n], raw_a.at[n], sem.at[n]) for n in range(3)]
        loads_b = []
        for n, half in enumerate(halves):
            loads_b.append(
                [pltpu.make_async_copy(src_own[s].at[half], raw_own.at[n, s], sem.at[3 + n * 7 + s]) for s in range(4)]
                + [pltpu.make_async_copy(src_near[s].at[half], raw_near.at[n, s], sem.at[7 + n * 7 + s]) for s in range(3)]
            )
        for copy in loads_a + loads_b[0]:
            copy.start()
        stores = []

        def store(source, target):
            stores.append(pltpu.make_async_copy(source, target, done.at[len(stores)]))
            stores[-1].start()

        steps = (0, 1, 3)
        for n, step in enumerate(steps):
            loads_a[n].wait()
            slot = (y - step * way) & 3
            for tile, value in laid_out(raw_a.at[n], rows):
                lanes = slice(tile % 4 * 128, tile % 4 * 128 + 128)
                a[slot, tile // 4, 0, :, lanes], a[slot, tile // 4, 1, :, lanes] = two_parts(value)
        store(a.at[y, z0], out_a[0])
        store(a.at[zh * 2 + 1 - yl, z0], out_a[1])
        for n, half in enumerate(halves):
            for copy in loads_b[n]:
                copy.wait()
            if n == 0:
                for copy in loads_b[1]:
                    copy.start()
            for s in range(4):
                slot = (z - s * way) & 3
                b[n, slot, 0, y], b[n, slot, 1, y] = two_parts(raw_own[n, s])
            for m, back in enumerate((1, 3, 2)):
                part = (y - back * way) & 3
                for k, step in enumerate(steps):
                    slot = (z - step * way) & 3
                    b[n, slot, 0, part], b[n, slot, 1, part] = two_parts(raw_near[n, k, m])
                empty = jnp.zeros((128, 512), BF16)
                b[n, (z + 2) & 3, 0, part], b[n, (z + 2) & 3, 1, part] = empty, empty
            store(b.at[n, pl.ds((1 - yh) * 2, 2)], out_b[n])
            for group, chosen in ((yl, (0,)), (1 - yl, (1, 3))):
                value = None
                for step in chosen:
                    slot = (y - step * way) & 3
                    for k in range(2):
                        bh, bl = (b[n, slot // 2 * 2 + k, p].reshape(512, 512) for p in range(2))
                        part = product(a[slot, k, 0], a[slot, k, 1], bh, bl)
                        value = part if value is None else value + part
                total[n, group] = value
            store(total.at[n], sums[n])
        for copy in stores:
            copy.wait()

    return pl.pallas_call(
        body,
        in_specs=[SMALL] + [ANY] * 10,
        out_specs=[ANY] * 6 + [pl.BlockSpec(memory_space=pltpu.VMEM)],
        out_shape=[jax.ShapeDtypeStruct((2, rows, 512), BF16)] * 2
        + [jax.ShapeDtypeStruct((2, 2, 4, 128, 512), BF16)] * 2
        + [jax.ShapeDtypeStruct((2, rows, 512), F32)] * 2
        + [jax.ShapeDtypeStruct((8, 128), F32)],
        scratch_shapes=[
            pltpu.VMEM((3, 8, rows, 128), F32),
            pltpu.VMEM((2, 4, 128, 512), F32),
            pltpu.VMEM((2, 3, 3, 128, 512), F32),
            pltpu.VMEM((4, 2, 2, rows, 512), BF16),
            pltpu.VMEM((2, 4, 2, 4, 128, 512), BF16),
            pltpu.VMEM((2, 2, rows, 512), F32),
            pltpu.SemaphoreType.DMA((17,)),
            pltpu.SemaphoreType.DMA((6,)),
        ],
        cost_estimate=pl.CostEstimate(flops=18 * rows * 2048 * 512, bytes_accessed=24 << 20, transcendentals=0),
        compiler_params=pltpu.CompilerParams(vmem_limit_bytes=VMEM_FIRST),
    )(place, *ints, *own, *near)


def last_products(place, sums, ints, near, own_a, other_a, far_b, ended):
    rows = sums.shape[1]

    def body(at, src_sum, src_far, src_near, src_own, src_other, src_b, unused, out, *refs):
        total, raw, raw_near, own, other, far, b, late, sem = refs
        half, z, y, core = at[0], at[1], at[2], at[3]
        way = 1 - 2 * core
        yl, yh = y & 1, y // 2
        zh, z0 = ((z + 2) & 3) // 2, z & 1
        pairs = (src_near.at[half], raw_near), (src_far, raw), (src_other, other), (src_sum, total), (src_own, own), (src_b, b)
        copies = [pltpu.make_async_copy(*pair, sem.at[n]) for n, pair in enumerate(pairs)]
        for copy in copies:
            copy.start()
        copies[0].wait()
        empty = jnp.zeros((128, 512), BF16)
        late[0, y], late[1, y] = empty, empty
        for m, back in enumerate((1, 3, 2)):
            slot = (y - back * way) & 3
            late[0, slot], late[1, slot] = two_parts(raw_near[m])
        bh, bl = late[0].reshape(512, 512), late[1].reshape(512, 512)
        copies[1].wait()
        for tile, value in laid_out(raw, rows):
            lanes = slice(tile % 4 * 128, tile % 4 * 128 + 128)
            far[tile // 4, 0, :, lanes], far[tile // 4, 1, :, lanes] = two_parts(value)
        for copy in copies[2:5]:
            copy.wait()
        value = total[1 - yl] + product(other[0], other[1], bh, bl)
        for x in range(4):
            out[(1 - yl) * 4 + x] = value[:, x * 128 : x * 128 + 128]

        @pl.when(yh != zh)
        def _():
            own[...] = far[z0]

        value = total[yl] + product(own[0], own[1], bh, bl)
        copies[5].wait()
        for k in range(2):
            value = value + product(far[k, 0], far[k, 1], *(b[k, p].reshape(512, 512) for p in range(2)))
        for x in range(4):
            out[yl * 4 + x] = value[:, x * 128 : x * 128 + 128]

    return pl.pallas_call(
        body,
        in_specs=[SMALL] + [ANY] * 7,
        out_specs=pl.BlockSpec(memory_space=pltpu.VMEM),
        out_shape=jax.ShapeDtypeStruct((8, rows, 128), F32),
        scratch_shapes=[
            pltpu.VMEM((2, rows, 512), F32),
            pltpu.VMEM((8, rows, 128), F32),
            pltpu.VMEM((3, 128, 512), F32),
            pltpu.VMEM((2, rows, 512), BF16),
            pltpu.VMEM((2, rows, 512), BF16),
            pltpu.VMEM((2, 2, rows, 512), BF16),
            pltpu.VMEM((2, 2, 4, 128, 512), BF16),
            pltpu.VMEM((2, 4, 128, 512), BF16),
            pltpu.SemaphoreType.DMA((6,)),
        ],
        cost_estimate=pl.CostEstimate(flops=6 * rows * 2048 * 512, bytes_accessed=8 << 20, transcendentals=0),
        compiler_params=pltpu.CompilerParams(vmem_limit_bytes=VMEM_LAST),
    )(place, sums, ints, near, own_a, other_a, far_b, ended)


def passed(ended):
    def body(a, b):
        b[...] = a[...]

    return pl.pallas_call(
        body,
        out_shape=jax.ShapeDtypeStruct(ended.shape, F32),
        cost_estimate=pl.CostEstimate(flops=12 * 10**9, bytes_accessed=8192, transcendentals=0),
        compiler_params=pltpu.CompilerParams(vmem_limit_bytes=4 << 20),
    )(ended)


def total_of(one, two):
    def body(a, b, out):
        out[...] = a[...] + b[...]

    whole = pl.BlockSpec(memory_space=pltpu.VMEM)
    return pl.pallas_call(
        body,
        in_specs=[whole] * 2,
        out_specs=whole,
        out_shape=jax.ShapeDtypeStruct(one.shape, F32),
        compiler_params=pltpu.CompilerParams(vmem_limit_bytes=4 << 20),
    )(one, two)


def finish(parts, driver, row_part, col_part):
    rows = driver.shape[0]

    def body(part, given, row, col, out):
        for yl in range(2):
            lanes = slice(yl * 128, (yl + 1) * 128)
            cycle = (part[yl * 4] + part[yl * 4 + 1]) + (part[yl * 4 + 2] + part[yl * 4 + 3])
            out[:, lanes] = (given[:, lanes] + cycle) / (row[...] + col[:, lanes])

    return pl.pallas_call(
        body,
        out_shape=jax.ShapeDtypeStruct((rows, 256), F32),
        compiler_params=pltpu.CompilerParams(vmem_limit_bytes=8 << 20),
    )(parts, driver, row_part, col_part)


def shards(integrals, amplitudes, driver, occ_rows, occ_cols, virtual):
    z, yl, yh, x, core = (lax.axis_index(axis) for axis in AXES)
    y = yh * 2 + yl
    way = 1 - 2 * core
    rows = driver.shape[0]
    number = lambda *v: jnp.stack([jnp.asarray(i, jnp.int32) for i in v])

    ints = split_integrals(integrals)
    amplitudes, ints = lax.optimization_barrier((amplitudes, ints))
    parts = split_amplitudes(amplitudes, number(*((y + d * way) % 4 for d in range(4))))
    on_z = lambda v, d: lax.ppermute(v, AXES, Z_ON[d])
    on_y = lambda v, d: lax.ppermute(v, AXES, Y_ON[d])
    wave = lambda *v: list(lax.optimization_barrier(v))
    ints = lax.all_to_all(ints, ("x", "core"), 0, 0, tiled=True)
    b = on_y(parts[1], 1)
    own2 = on_z(parts[0], 2)
    d = on_y(parts[2], 2)
    own1 = on_z(parts[0], 1)
    c = on_y(parts[3], 3)
    own3 = on_z(parts[0], 3)
    own = [parts[0], own1, own2, own3]
    ints, b, c, d, *own[1:] = wave(ints, b, c, d, *own[1:])
    bcd = jnp.stack([b, c, d], axis=1)
    bcd1, bcd3 = on_z(bcd, 1), on_z(bcd, 3)
    ints1, ints3 = on_y(ints, 1), on_y(ints, 3)
    bcd2, ints2 = on_z(bcd1, 1), on_y(ints1, 1)
    own_a, other_a, far_other, far_mine, sum_other, sum_mine, ended = first_products(
        number(core, z, y), (ints, ints1, ints3), own, (bcd, bcd1, bcd3)
    )
    bcd2, ints2, ended = wave(bcd2, ints2, passed(ended))
    other = last_products(number(1 - core, z, y, core), sum_other, ints2, bcd2, own_a, other_a, far_other, ended)
    mine = last_products(number(core, z, y, core), sum_mine, ints2, bcd2, own_a, other_a, far_mine, ended)
    mine = total_of(mine, lax.ppermute(other, AXES, SWAP))
    mine = lax.all_to_all(mine, ("yl", "x"), 0, 0, tiled=True)
    row_energy = (occ_rows[:, None] - virtual[None, :]).reshape(-1)
    col_energy = (occ_cols[:, None] - virtual[None, :]).reshape(-1)
    row_part = lax.dynamic_slice_in_dim(row_energy, (z * 2 + yl) * rows, rows, 0)
    col_part = lax.dynamic_slice_in_dim(col_energy, ((yh * 4 + x) * 2 + core) * 256, 256, 0)
    return finish(mine, driver, row_part[:, None], col_part[None, :])


def solution(mesh):
    fine = Mesh(mesh.devices.reshape(SIZES), AXES)
    row, col = ("z", "yl"), ("yh", "x", "core")
    in_specs = (P(row, col), P(row, col, None, None), P(row, col), P(), P(), P())
    return jax.shard_map(shards, mesh=fine, in_specs=in_specs, out_specs=P(row, col), check_vma=False)
```

```python
import functools

import jax
import jax.numpy as jnp
from jax import lax
from jax.experimental import pallas as pl
from jax.experimental.pallas import tpu as pltpu
from jax.sharding import Mesh, PartitionSpec as P

AXES = ("z", "yl", "yh", "x", "core")
SIZES = (4, 2, 2, 4, 2)
F32, BF16 = jnp.float32, jnp.bfloat16


def device_index(z, y, x, core):
    return (((z * 2 + y % 2) * 2 + y // 2) * 4 + x) * 2 + core


def moves(target):
    pairs = []
    for z in range(4):
        for y in range(4):
            for x in range(4):
                for core in range(2):
                    pairs.append((device_index(z, y, x, core), device_index(*target(z, y, x, core))))
    return pairs


Z_ON = [moves(lambda z, y, x, core, d=d: ((z + d * (1 - 2 * core)) % 4, y, x, core)) for d in range(4)]
Y_ON = [moves(lambda z, y, x, core, d=d: (z, (y + d * (1 - 2 * core)) % 4, x, core)) for d in range(4)]
SWAP = moves(lambda z, y, x, core: (z, y, x, 1 - core))


def call(body, grid, in_specs, out_specs, out_shape, scalars, operands, scratch=(), aliases=None, flops=0, vmem=8 << 20):
    nbytes = sum(4 * o.size for o in operands[:1])
    return pl.pallas_call(
        body,
        grid_spec=pltpu.PrefetchScalarGridSpec(
            num_scalar_prefetch=1, grid=grid, in_specs=in_specs, out_specs=out_specs, scratch_shapes=list(scratch)
        ),
        out_shape=out_shape,
        input_output_aliases=aliases or {},
        cost_estimate=pl.CostEstimate(flops=flops, bytes_accessed=2 * nbytes, transcendentals=0),
        compiler_params=pltpu.CompilerParams(vmem_limit_bytes=vmem),
    )(scalars, *operands)


def split_amplitudes(amplitudes, targets):
    def body(target, src, *refs):
        outs, turned = refs[:4], refs[4]
        turned[...] = jnp.swapaxes(src[0], 0, 1)
        for out, slot in zip(outs, range(4)):
            y = target[slot]
            yh, yl = y // 2, y % 2
            for half in range(2):
                lanes = pl.ds(pl.multiple_of(half * 256 + yl * 128, 128), 128)
                for x in range(4):
                    out[half, :, x * 128 : (x + 1) * 128] = turned[yh * 4 + x, :, lanes]

    return call(
        body,
        (4,),
        [pl.BlockSpec((1, 32, 8, 512), lambda k, t: (k, 0, 0, 0))],
        [pl.BlockSpec((2, 32, 512), lambda k, t: (0, k, 0))] * 4,
        [jax.ShapeDtypeStruct((2, 128, 512), F32)] * 4,
        targets,
        (amplitudes,),
        scratch=[pltpu.VMEM((8, 32, 512), F32)],
    )


def split_integrals(integrals):
    rows = integrals.shape[0]
    step = rows // 3

    def body(unused, src, out):
        lane = lax.broadcasted_iota(jnp.int32, (step, 128), 1) // 32
        for h in range(2):
            tiles = [src[:, (e * 4 + yh * 2 + h) * 128 :][:, :128] for yh in range(2) for e in range(2)]
            for j in range(4):
                made = None
                for s in range(4):
                    turn = (s - j) % 4 * 32
                    moved = pltpu.roll(tiles[s], turn, 1) if turn else tiles[s]
                    made = moved if made is None else jnp.where(lane == s, moved, made)
                out[h * 4 + j] = made

    return call(
        body,
        (3,),
        [pl.BlockSpec((step, 1024), lambda r, t: (r, 0))],
        pl.BlockSpec((8, step, 128), lambda r, t: (0, r, 0)),
        jax.ShapeDtypeStruct((8, rows, 128), F32),
        jnp.zeros((1,), jnp.int32),
        (integrals,),
    )


def two_parts(value):
    high = value.astype(BF16)
    return high, (value - high.astype(F32)).astype(BF16)


def laid_out(src, rows):
    first = lax.broadcasted_iota(jnp.int32, (rows, 128), 1) < 64
    for z0 in range(src.shape[0] // 4):
        for yb in range(2):
            one, two = src[z0 * 4 + yb * 2], src[z0 * 4 + yb * 2 + 1]
            yield (z0 * 2 + 0) * 2 + yb, jnp.where(first, one, pltpu.roll(two, 64, 1))
            yield (z0 * 2 + 1) * 2 + yb, jnp.where(first, pltpu.roll(one, 64, 1), two)


def product(ah, al, bh, bl):
    dot = functools.partial(jnp.dot, preferred_element_type=F32)
    return dot(ah, bh) + (dot(ah, bl) + dot(al, bh))


ANY = pl.BlockSpec(memory_space=pl.ANY)
VMEM_FIRST, VMEM_LAST = 56 << 20, 20 << 20
SMALL = pl.BlockSpec(memory_space=pltpu.SMEM)


def first_products(place, ints, own, near):
    rows = ints[0].shape[1]

    def body(at, *refs):
        src_a, src_own, src_near = refs[:3], refs[3:7], refs[7:10]
        out_a, out_b, sums = refs[10:12], refs[12:14], refs[14:16]
        raw_a, raw_own, raw_near, a, b, total, sem, done = refs[17:]
        refs[16][...] = jnp.zeros((8, 128), F32)
        core, z, y = at[0], at[1], at[2]
        way = 1 - 2 * core
        yl, yh = y & 1, y // 2
        zh, z0 = ((z + 2) & 3) // 2, z & 1
        halves = (1 - core, core)
        loads_a = [pltpu.make_async_copy(src_a[n], raw_a.at[n], sem.at[n]) for n in range(3)]
        loads_b = []
        for n, half in enumerate(halves):
            loads_b.append(
                [pltpu.make_async_copy(src_own[s].at[half], raw_own.at[n, s], sem.at[3 + n * 7 + s]) for s in range(4)]
                + [pltpu.make_async_copy(src_near[s].at[half], raw_near.at[n, s], sem.at[7 + n * 7 + s]) for s in range(3)]
            )
        for copy in loads_a + loads_b[0]:
            copy.start()
        stores = []

        def store(source, target):
            stores.append(pltpu.make_async_copy(source, target, done.at[len(stores)]))
            stores[-1].start()

        steps = (0, 1, 3)
        for n, step in enumerate(steps):
            loads_a[n].wait()
            slot = (y - step * way) & 3
            for tile, value in laid_out(raw_a.at[n], rows):
                lanes = slice(tile % 4 * 128, tile % 4 * 128 + 128)
                a[slot, tile // 4, 0, :, lanes], a[slot, tile // 4, 1, :, lanes] = two_parts(value)
        store(a.at[y, z0], out_a[0])
        store(a.at[zh * 2 + 1 - yl, z0], out_a[1])
        for n, half in enumerate(halves):
            for copy in loads_b[n]:
                copy.wait()
            if n == 0:
                for copy in loads_b[1]:
                    copy.start()
            for s in range(4):
                slot = (z - s * way) & 3
                b[n, slot, 0, y], b[n, slot, 1, y] = two_parts(raw_own[n, s])
            for m, back in enumerate((1, 3, 2)):
                part = (y - back * way) & 3
                for k, step in enumerate(steps):
                    slot = (z - step * way) & 3
                    b[n, slot, 0, part], b[n, slot, 1, part] = two_parts(raw_near[n, k, m])
                empty = jnp.zeros((128, 512), BF16)
                b[n, (z + 2) & 3, 0, part], b[n, (z + 2) & 3, 1, part] = empty, empty
            store(b.at[n, pl.ds((1 - yh) * 2, 2)], out_b[n])
            for group, chosen in ((yl, (0,)), (1 - yl, (1, 3))):
                value = None
                for step in chosen:
                    slot = (y - step * way) & 3
                    for k in range(2):
                        bh, bl = (b[n, slot // 2 * 2 + k, p].reshape(512, 512) for p in range(2))
                        part = product(a[slot, k, 0], a[slot, k, 1], bh, bl)
                        value = part if value is None else value + part
                total[n, group] = value
            store(total.at[n], sums[n])
        for copy in stores:
            copy.wait()

    return pl.pallas_call(
        body,
        in_specs=[SMALL] + [ANY] * 10,
        out_specs=[ANY] * 6 + [pl.BlockSpec(memory_space=pltpu.VMEM)],
        out_shape=[jax.ShapeDtypeStruct((2, rows, 512), BF16)] * 2
        + [jax.ShapeDtypeStruct((2, 2, 4, 128, 512), BF16)] * 2
        + [jax.ShapeDtypeStruct((2, rows, 512), F32)] * 2
        + [jax.ShapeDtypeStruct((8, 128), F32)],
        scratch_shapes=[
            pltpu.VMEM((3, 8, rows, 128), F32),
            pltpu.VMEM((2, 4, 128, 512), F32),
            pltpu.VMEM((2, 3, 3, 128, 512), F32),
            pltpu.VMEM((4, 2, 2, rows, 512), BF16),
            pltpu.VMEM((2, 4, 2, 4, 128, 512), BF16),
            pltpu.VMEM((2, 2, rows, 512), F32),
            pltpu.SemaphoreType.DMA((17,)),
            pltpu.SemaphoreType.DMA((6,)),
        ],
        cost_estimate=pl.CostEstimate(flops=18 * rows * 2048 * 512, bytes_accessed=24 << 20, transcendentals=0),
        compiler_params=pltpu.CompilerParams(vmem_limit_bytes=VMEM_FIRST),
    )(place, *ints, *own, *near)


def last_products(place, sums, ints, near, own_a, other_a, far_b, ended):
    rows = sums.shape[1]

    def body(at, src_sum, src_far, src_near, src_own, src_other, src_b, unused, out, *refs):
        total, raw, raw_near, own, other, far, b, late, sem = refs
        half, z, y, core = at[0], at[1], at[2], at[3]
        way = 1 - 2 * core
        yl, yh = y & 1, y // 2
        zh, z0 = ((z + 2) & 3) // 2, z & 1
        pairs = (src_near.at[half], raw_near), (src_far, raw), (src_other, other), (src_sum, total), (src_own, own), (src_b, b)
        copies = [pltpu.make_async_copy(*pair, sem.at[n]) for n, pair in enumerate(pairs)]
        for copy in copies:
            copy.start()
        copies[0].wait()
        empty = jnp.zeros((128, 512), BF16)
        late[0, y], late[1, y] = empty, empty
        for m, back in enumerate((1, 3, 2)):
            slot = (y - back * way) & 3
            late[0, slot], late[1, slot] = two_parts(raw_near[m])
        bh, bl = late[0].reshape(512, 512), late[1].reshape(512, 512)
        copies[1].wait()
        for tile, value in laid_out(raw, rows):
            lanes = slice(tile % 4 * 128, tile % 4 * 128 + 128)
            far[tile // 4, 0, :, lanes], far[tile // 4, 1, :, lanes] = two_parts(value)
        for copy in copies[2:5]:
            copy.wait()
        value = total[1 - yl] + product(other[0], other[1], bh, bl)
        for x in range(4):
            out[(1 - yl) * 4 + x] = value[:, x * 128 : x * 128 + 128]

        @pl.when(yh != zh)
        def _():
            own[...] = far[z0]

        value = total[yl] + product(own[0], own[1], bh, bl)
        copies[5].wait()
        for k in range(2):
            value = value + product(far[k, 0], far[k, 1], *(b[k, p].reshape(512, 512) for p in range(2)))
        for x in range(4):
            out[yl * 4 + x] = value[:, x * 128 : x * 128 + 128]

    return pl.pallas_call(
        body,
        in_specs=[SMALL] + [ANY] * 7,
        out_specs=pl.BlockSpec(memory_space=pltpu.VMEM),
        out_shape=jax.ShapeDtypeStruct((8, rows, 128), F32),
        scratch_shapes=[
            pltpu.VMEM((2, rows, 512), F32),
            pltpu.VMEM((8, rows, 128), F32),
            pltpu.VMEM((3, 128, 512), F32),
            pltpu.VMEM((2, rows, 512), BF16),
            pltpu.VMEM((2, rows, 512), BF16),
            pltpu.VMEM((2, 2, rows, 512), BF16),
            pltpu.VMEM((2, 2, 4, 128, 512), BF16),
            pltpu.VMEM((2, 4, 128, 512), BF16),
            pltpu.SemaphoreType.DMA((6,)),
        ],
        cost_estimate=pl.CostEstimate(flops=6 * rows * 2048 * 512, bytes_accessed=8 << 20, transcendentals=0),
        compiler_params=pltpu.CompilerParams(vmem_limit_bytes=VMEM_LAST),
    )(place, sums, ints, near, own_a, other_a, far_b, ended)


def passed(ended):
    def body(a, b):
        b[...] = a[...]

    return pl.pallas_call(
        body,
        out_shape=jax.ShapeDtypeStruct(ended.shape, F32),
        cost_estimate=pl.CostEstimate(flops=12 * 10**9, bytes_accessed=8192, transcendentals=0),
        compiler_params=pltpu.CompilerParams(vmem_limit_bytes=4 << 20),
    )(ended)


def total_of(one, two):
    def body(a, b, out):
        out[...] = a[...] + b[...]

    whole = pl.BlockSpec(memory_space=pltpu.VMEM)
    return pl.pallas_call(
        body,
        in_specs=[whole] * 2,
        out_specs=whole,
        out_shape=jax.ShapeDtypeStruct(one.shape, F32),
        compiler_params=pltpu.CompilerParams(vmem_limit_bytes=4 << 20),
    )(one, two)


def finish(parts, driver, row_part, col_part):
    rows = driver.shape[0]

    def body(part, given, row, col, out):
        for yl in range(2):
            lanes = slice(yl * 128, (yl + 1) * 128)
            cycle = (part[yl * 4] + part[yl * 4 + 1]) + (part[yl * 4 + 2] + part[yl * 4 + 3])
            out[:, lanes] = (given[:, lanes] + cycle) / (row[...] + col[:, lanes])

    return pl.pallas_call(
        body,
        out_shape=jax.ShapeDtypeStruct((rows, 256), F32),
        compiler_params=pltpu.CompilerParams(vmem_limit_bytes=8 << 20),
    )(parts, driver, row_part, col_part)


def shards(integrals, amplitudes, driver, occ_rows, occ_cols, virtual):
    z, yl, yh, x, core = (lax.axis_index(axis) for axis in AXES)
    y = yh * 2 + yl
    way = 1 - 2 * core
    rows = driver.shape[0]
    number = lambda *v: jnp.stack([jnp.asarray(i, jnp.int32) for i in v])

    ints = split_integrals(integrals)
    amplitudes, ints = lax.optimization_barrier((amplitudes, ints))
    parts = split_amplitudes(amplitudes, number(*((y + d * way) % 4 for d in range(4))))
    on_z = lambda v, d: lax.ppermute(v, AXES, Z_ON[d])
    on_y = lambda v, d: lax.ppermute(v, AXES, Y_ON[d])
    wave = lambda *v: list(lax.optimization_barrier(v))
    ints = lax.all_to_all(ints, ("x", "core"), 0, 0, tiled=True)
    b, d, c = on_y(parts[1], 1), on_y(parts[2], 2), on_y(parts[3], 3)
    own1, own3 = on_z(parts[0], 1), on_z(parts[0], 3)
    own2 = on_z(own1, 1)
    ints, own1, b, own3, d, c, own2 = wave(ints, own1, b, own3, d, c, own2)
    own = [parts[0], own1, own2, own3]
    bcd = jnp.stack([b, c, d], axis=1)
    bcd1, bcd3 = on_z(bcd, 1), on_z(bcd, 3)
    ints1, ints3 = on_y(ints, 1), on_y(ints, 3)
    bcd2, ints2 = on_z(bcd1, 1), on_y(ints1, 1)
    own_a, other_a, far_other, far_mine, sum_other, sum_mine, ended = first_products(
        number(core, z, y), (ints, ints1, ints3), own, (bcd, bcd1, bcd3)
    )
    bcd2, ints2, ended = wave(bcd2, ints2, passed(ended))
    other = last_products(number(1 - core, z, y, core), sum_other, ints2, bcd2, own_a, other_a, far_other, ended)
    mine = last_products(number(core, z, y, core), sum_mine, ints2, bcd2, own_a, other_a, far_mine, ended)
    mine = total_of(mine, lax.ppermute(other, AXES, SWAP))
    mine = lax.all_to_all(mine, ("yl", "x"), 0, 0, tiled=True)
    row_energy = (occ_rows[:, None] - virtual[None, :]).reshape(-1)
    col_energy = (occ_cols[:, None] - virtual[None, :]).reshape(-1)
    row_part = lax.dynamic_slice_in_dim(row_energy, (z * 2 + yl) * rows, rows, 0)
    col_part = lax.dynamic_slice_in_dim(col_energy, ((yh * 4 + x) * 2 + core) * 256, 256, 0)
    return finish(mine, driver, row_part[:, None], col_part[None, :])


def solution(mesh):
    fine = Mesh(mesh.devices.reshape(SIZES), AXES)
    row, col = ("z", "yl"), ("yh", "x", "core")
    in_specs = (P(row, col), P(row, col, None, None), P(row, col), P(), P(), P())
    return jax.shard_map(shards, mesh=fine, in_specs=in_specs, out_specs=P(row, col), check_vma=False)
```

```python
import functools

import jax
import jax.numpy as jnp
from jax import lax
from jax.experimental import pallas as pl
from jax.experimental.pallas import tpu as pltpu
from jax.sharding import Mesh, PartitionSpec as P

AXES = ("z", "yl", "yh", "x", "core")
SIZES = (4, 2, 2, 4, 2)
F32, BF16 = jnp.float32, jnp.bfloat16


def device_index(z, y, x, core):
    return (((z * 2 + y % 2) * 2 + y // 2) * 4 + x) * 2 + core


def moves(target):
    pairs = []
    for z in range(4):
        for y in range(4):
            for x in range(4):
                for core in range(2):
                    pairs.append((device_index(z, y, x, core), device_index(*target(z, y, x, core))))
    return pairs


Z_ON = [moves(lambda z, y, x, core, d=d: ((z + d * (1 - 2 * core)) % 4, y, x, core)) for d in range(4)]
Y_ON = [moves(lambda z, y, x, core, d=d: (z, (y + d * (1 - 2 * core)) % 4, x, core)) for d in range(4)]
SWAP = moves(lambda z, y, x, core: (z, y, x, 1 - core))


def call(body, grid, in_specs, out_specs, out_shape, scalars, operands, scratch=(), aliases=None, flops=0, vmem=8 << 20):
    nbytes = sum(4 * o.size for o in operands[:1])
    return pl.pallas_call(
        body,
        grid_spec=pltpu.PrefetchScalarGridSpec(
            num_scalar_prefetch=1, grid=grid, in_specs=in_specs, out_specs=out_specs, scratch_shapes=list(scratch)
        ),
        out_shape=out_shape,
        input_output_aliases=aliases or {},
        cost_estimate=pl.CostEstimate(flops=flops, bytes_accessed=2 * nbytes, transcendentals=0),
        compiler_params=pltpu.CompilerParams(vmem_limit_bytes=vmem),
    )(scalars, *operands)


def split_amplitudes(amplitudes, targets):
    def body(target, src, *refs):
        outs, turned = refs[:4], refs[4]
        turned[...] = jnp.swapaxes(src[0], 0, 1)
        for out, slot in zip(outs, range(4)):
            y = target[slot]
            yh, yl = y // 2, y % 2
            for half in range(2):
                lanes = pl.ds(pl.multiple_of(half * 256 + yl * 128, 128), 128)
                for x in range(4):
                    out[half, :, x * 128 : (x + 1) * 128] = turned[yh * 4 + x, :, lanes]

    return call(
        body,
        (4,),
        [pl.BlockSpec((1, 32, 8, 512), lambda k, t: (k, 0, 0, 0))],
        [pl.BlockSpec((2, 32, 512), lambda k, t: (0, k, 0))] * 4,
        [jax.ShapeDtypeStruct((2, 128, 512), F32)] * 4,
        targets,
        (amplitudes,),
        scratch=[pltpu.VMEM((8, 32, 512), F32)],
    )


def split_integrals(integrals):
    rows = integrals.shape[0]
    step = rows // 3

    def body(unused, src, out):
        lane = lax.broadcasted_iota(jnp.int32, (step, 128), 1) // 32
        for h in range(2):
            tiles = [src[:, (e * 4 + yh * 2 + h) * 128 :][:, :128] for yh in range(2) for e in range(2)]
            for j in range(4):
                made = None
                for s in range(4):
                    turn = (s - j) % 4 * 32
                    moved = pltpu.roll(tiles[s], turn, 1) if turn else tiles[s]
                    made = moved if made is None else jnp.where(lane == s, moved, made)
                out[h * 4 + j] = made

    return call(
        body,
        (3,),
        [pl.BlockSpec((step, 1024), lambda r, t: (r, 0))],
        pl.BlockSpec((8, step, 128), lambda r, t: (0, r, 0)),
        jax.ShapeDtypeStruct((8, rows, 128), F32),
        jnp.zeros((1,), jnp.int32),
        (integrals,),
    )


def two_parts(value):
    high = value.astype(BF16)
    return high, (value - high.astype(F32)).astype(BF16)


def laid_out(src, rows):
    first = lax.broadcasted_iota(jnp.int32, (rows, 128), 1) < 64
    for z0 in range(src.shape[0] // 4):
        for yb in range(2):
            one, two = src[z0 * 4 + yb * 2], src[z0 * 4 + yb * 2 + 1]
            yield (z0 * 2 + 0) * 2 + yb, jnp.where(first, one, pltpu.roll(two, 64, 1))
            yield (z0 * 2 + 1) * 2 + yb, jnp.where(first, pltpu.roll(one, 64, 1), two)


def product(ah, al, bh, bl):
    dot = functools.partial(jnp.dot, preferred_element_type=F32)
    return dot(ah, bh) + (dot(ah, bl) + dot(al, bh))


ANY = pl.BlockSpec(memory_space=pl.ANY)
VMEM_FIRST, VMEM_LAST = 56 << 20, 20 << 20
SMALL = pl.BlockSpec(memory_space=pltpu.SMEM)


def first_products(place, ints, own, near):
    rows = ints[0].shape[1]

    def body(at, *refs):
        src_a, src_own, src_near = refs[:3], refs[3:7], refs[7:10]
        out_a, out_b, sums = refs[10:12], refs[12:14], refs[14:16]
        raw_a, raw_own, raw_near, a, b, total, sem, done = refs[17:]
        refs[16][...] = jnp.zeros((8, 128), F32)
        core, z, y = at[0], at[1], at[2]
        way = 1 - 2 * core
        yl, yh = y & 1, y // 2
        zh, z0 = ((z + 2) & 3) // 2, z & 1
        halves = (1 - core, core)
        loads_a = [pltpu.make_async_copy(src_a[n], raw_a.at[n], sem.at[n]) for n in range(3)]
        loads_b = []
        for n, half in enumerate(halves):
            loads_b.append(
                [pltpu.make_async_copy(src_own[s].at[half], raw_own.at[n, s], sem.at[3 + n * 7 + s]) for s in range(4)]
                + [pltpu.make_async_copy(src_near[s].at[half], raw_near.at[n, s], sem.at[7 + n * 7 + s]) for s in range(3)]
            )
        for copy in loads_a + loads_b[0]:
            copy.start()
        stores = []

        def store(source, target):
            stores.append(pltpu.make_async_copy(source, target, done.at[len(stores)]))
            stores[-1].start()

        steps = (0, 1, 3)
        for n, step in enumerate(steps):
            loads_a[n].wait()
            slot = (y - step * way) & 3
            for tile, value in laid_out(raw_a.at[n], rows):
                lanes = slice(tile % 4 * 128, tile % 4 * 128 + 128)
                a[slot, tile // 4, 0, :, lanes], a[slot, tile // 4, 1, :, lanes] = two_parts(value)
        store(a.at[y, z0], out_a[0])
        store(a.at[zh * 2 + 1 - yl, z0], out_a[1])
        for n, half in enumerate(halves):
            for copy in loads_b[n]:
                copy.wait()
            if n == 0:
                for copy in loads_b[1]:
                    copy.start()
            for s in range(4):
                slot = (z - s * way) & 3
                b[n, slot, 0, y], b[n, slot, 1, y] = two_parts(raw_own[n, s])
            for m, back in enumerate((1, 3, 2)):
                part = (y - back * way) & 3
                for k, step in enumerate(steps):
                    slot = (z - step * way) & 3
                    b[n, slot, 0, part], b[n, slot, 1, part] = two_parts(raw_near[n, k, m])
                empty = jnp.zeros((128, 512), BF16)
                b[n, (z + 2) & 3, 0, part], b[n, (z + 2) & 3, 1, part] = empty, empty
            store(b.at[n, pl.ds((1 - yh) * 2, 2)], out_b[n])
            for group, chosen in ((yl, (0,)), (1 - yl, (1, 3))):
                value = None
                for step in chosen:
                    slot = (y - step * way) & 3
                    for k in range(2):
                        bh, bl = (b[n, slot // 2 * 2 + k, p].reshape(512, 512) for p in range(2))
                        part = product(a[slot, k, 0], a[slot, k, 1], bh, bl)
                        value = part if value is None else value + part
                total[n, group] = value
            store(total.at[n], sums[n])
        for copy in stores:
            copy.wait()

    return pl.pallas_call(
        body,
        in_specs=[SMALL] + [ANY] * 10,
        out_specs=[ANY] * 6 + [pl.BlockSpec(memory_space=pltpu.VMEM)],
        out_shape=[jax.ShapeDtypeStruct((2, rows, 512), BF16)] * 2
        + [jax.ShapeDtypeStruct((2, 2, 4, 128, 512), BF16)] * 2
        + [jax.ShapeDtypeStruct((2, rows, 512), F32)] * 2
        + [jax.ShapeDtypeStruct((8, 128), F32)],
        scratch_shapes=[
            pltpu.VMEM((3, 8, rows, 128), F32),
            pltpu.VMEM((2, 4, 128, 512), F32),
            pltpu.VMEM((2, 3, 3, 128, 512), F32),
            pltpu.VMEM((4, 2, 2, rows, 512), BF16),
            pltpu.VMEM((2, 4, 2, 4, 128, 512), BF16),
            pltpu.VMEM((2, 2, rows, 512), F32),
            pltpu.SemaphoreType.DMA((17,)),
            pltpu.SemaphoreType.DMA((6,)),
        ],
        cost_estimate=pl.CostEstimate(flops=18 * rows * 2048 * 512, bytes_accessed=24 << 20, transcendentals=0),
        compiler_params=pltpu.CompilerParams(vmem_limit_bytes=VMEM_FIRST),
    )(place, *ints, *own, *near)


def last_products(place, sums, ints, near, own_a, other_a, far_b, ended):
    rows = sums.shape[1]

    def body(at, src_sum, src_far, src_near, src_own, src_other, src_b, unused, out, *refs):
        total, raw, raw_near, own, other, far, b, late, sem = refs
        half, z, y, core = at[0], at[1], at[2], at[3]
        way = 1 - 2 * core
        yl, yh = y & 1, y // 2
        zh, z0 = ((z + 2) & 3) // 2, z & 1
        pairs = (src_near.at[half], raw_near), (src_far, raw), (src_other, other), (src_sum, total), (src_own, own), (src_b, b)
        copies = [pltpu.make_async_copy(*pair, sem.at[n]) for n, pair in enumerate(pairs)]
        for copy in copies:
            copy.start()
        copies[0].wait()
        empty = jnp.zeros((128, 512), BF16)
        late[0, y], late[1, y] = empty, empty
        for m, back in enumerate((1, 3, 2)):
            slot = (y - back * way) & 3
            late[0, slot], late[1, slot] = two_parts(raw_near[m])
        bh, bl = late[0].reshape(512, 512), late[1].reshape(512, 512)
        copies[1].wait()
        for tile, value in laid_out(raw, rows):
            lanes = slice(tile % 4 * 128, tile % 4 * 128 + 128)
            far[tile // 4, 0, :, lanes], far[tile // 4, 1, :, lanes] = two_parts(value)
        for copy in copies[2:5]:
            copy.wait()
        value = total[1 - yl] + product(other[0], other[1], bh, bl)
        for x in range(4):
            out[(1 - yl) * 4 + x] = value[:, x * 128 : x * 128 + 128]

        @pl.when(yh != zh)
        def _():
            own[...] = far[z0]

        value = total[yl] + product(own[0], own[1], bh, bl)
        copies[5].wait()
        for k in range(2):
            value = value + product(far[k, 0], far[k, 1], *(b[k, p].reshape(512, 512) for p in range(2)))
        for x in range(4):
            out[yl * 4 + x] = value[:, x * 128 : x * 128 + 128]

    return pl.pallas_call(
        body,
        in_specs=[SMALL] + [ANY] * 7,
        out_specs=pl.BlockSpec(memory_space=pltpu.VMEM),
        out_shape=jax.ShapeDtypeStruct((8, rows, 128), F32),
        scratch_shapes=[
            pltpu.VMEM((2, rows, 512), F32),
            pltpu.VMEM((8, rows, 128), F32),
            pltpu.VMEM((3, 128, 512), F32),
            pltpu.VMEM((2, rows, 512), BF16),
            pltpu.VMEM((2, rows, 512), BF16),
            pltpu.VMEM((2, 2, rows, 512), BF16),
            pltpu.VMEM((2, 2, 4, 128, 512), BF16),
            pltpu.VMEM((2, 4, 128, 512), BF16),
            pltpu.SemaphoreType.DMA((6,)),
        ],
        cost_estimate=pl.CostEstimate(flops=6 * rows * 2048 * 512, bytes_accessed=8 << 20, transcendentals=0),
        compiler_params=pltpu.CompilerParams(vmem_limit_bytes=VMEM_LAST),
    )(place, sums, ints, near, own_a, other_a, far_b, ended)


def passed(ended):
    def body(a, b):
        b[...] = a[...]

    return pl.pallas_call(
        body,
        out_shape=jax.ShapeDtypeStruct(ended.shape, F32),
        cost_estimate=pl.CostEstimate(flops=12 * 10**9, bytes_accessed=8192, transcendentals=0),
        compiler_params=pltpu.CompilerParams(vmem_limit_bytes=4 << 20),
    )(ended)


def total_of(one, two):
    def body(a, b, out):
        out[...] = a[...] + b[...]

    whole = pl.BlockSpec(memory_space=pltpu.VMEM)
    return pl.pallas_call(
        body,
        in_specs=[whole] * 2,
        out_specs=whole,
        out_shape=jax.ShapeDtypeStruct(one.shape, F32),
        compiler_params=pltpu.CompilerParams(vmem_limit_bytes=4 << 20),
    )(one, two)


def finish(parts, driver, row_part, col_part):
    rows = driver.shape[0]

    def body(part, given, row, col, out):
        for yl in range(2):
            lanes = slice(yl * 128, (yl + 1) * 128)
            cycle = (part[yl * 4] + part[yl * 4 + 1]) + (part[yl * 4 + 2] + part[yl * 4 + 3])
            out[:, lanes] = (given[:, lanes] + cycle) / (row[...] + col[:, lanes])

    return pl.pallas_call(
        body,
        out_shape=jax.ShapeDtypeStruct((rows, 256), F32),
        compiler_params=pltpu.CompilerParams(vmem_limit_bytes=8 << 20),
    )(parts, driver, row_part, col_part)


def shards(integrals, amplitudes, driver, occ_rows, occ_cols, virtual):
    z, yl, yh, x, core = (lax.axis_index(axis) for axis in AXES)
    y = yh * 2 + yl
    way = 1 - 2 * core
    rows = driver.shape[0]
    number = lambda *v: jnp.stack([jnp.asarray(i, jnp.int32) for i in v])

    ints = split_integrals(integrals)
    amplitudes, ints = lax.optimization_barrier((amplitudes, ints))
    parts = split_amplitudes(amplitudes, number(*((y + d * way) % 4 for d in range(4))))
    on_z = lambda v, d: lax.ppermute(v, AXES, Z_ON[d])
    on_y = lambda v, d: lax.ppermute(v, AXES, Y_ON[d])
    wave = lambda *v: list(lax.optimization_barrier(v))
    ints = lax.all_to_all(ints, ("x", "core"), 0, 0, tiled=True)
    b, d, c = on_y(parts[1], 1), on_y(parts[2], 2), on_y(parts[3], 3)
    own1 = on_z(parts[0], 1)
    own3 = on_z(wave(parts[0], own1)[0], 3)
    own2 = on_z(own1, 1)
    ints, b, own1, d, own3, c, own2 = wave(ints, b, own1, d, own3, c, own2)
    own = [parts[0], own1, own2, own3]
    bcd = jnp.stack([b, c, d], axis=1)
    bcd1, bcd3 = on_z(bcd, 1), on_z(bcd, 3)
    ints1, ints3 = on_y(ints, 1), on_y(ints, 3)
    bcd2, ints2 = on_z(bcd1, 1), on_y(ints1, 1)
    own_a, other_a, far_other, far_mine, sum_other, sum_mine, ended = first_products(
        number(core, z, y), (ints, ints1, ints3), own, (bcd, bcd1, bcd3)
    )
    bcd2, ints2, ended = wave(bcd2, ints2, passed(ended))
    other = last_products(number(1 - core, z, y, core), sum_other, ints2, bcd2, own_a, other_a, far_other, ended)
    mine = last_products(number(core, z, y, core), sum_mine, ints2, bcd2, own_a, other_a, far_mine, ended)
    mine = total_of(mine, lax.ppermute(other, AXES, SWAP))
    mine = lax.all_to_all(mine, ("yl", "x"), 0, 0, tiled=True)
    row_energy = (occ_rows[:, None] - virtual[None, :]).reshape(-1)
    col_energy = (occ_cols[:, None] - virtual[None, :]).reshape(-1)
    row_part = lax.dynamic_slice_in_dim(row_energy, (z * 2 + yl) * rows, rows, 0)
    col_part = lax.dynamic_slice_in_dim(col_energy, ((yh * 4 + x) * 2 + core) * 256, 256, 0)
    return finish(mine, driver, row_part[:, None], col_part[None, :])


def solution(mesh):
    fine = Mesh(mesh.devices.reshape(SIZES), AXES)
    row, col = ("z", "yl"), ("yh", "x", "core")
    in_specs = (P(row, col), P(row, col, None, None), P(row, col), P(), P(), P())
    return jax.shard_map(shards, mesh=fine, in_specs=in_specs, out_specs=P(row, col), check_vma=False)
```

```python
import functools

import jax
import jax.numpy as jnp
from jax import lax
from jax.experimental import pallas as pl
from jax.experimental.pallas import tpu as pltpu
from jax.sharding import Mesh, PartitionSpec as P

AXES = ("z", "yl", "yh", "xh", "xl", "core")
SIZES = (4, 2, 2, 2, 2, 2)
F32, BF16 = jnp.float32, jnp.bfloat16


def device_index(z, y, x, core):
    return (((z * 2 + y % 2) * 2 + y // 2) * 4 + x) * 2 + core


def moves(target):
    pairs = []
    for z in range(4):
        for y in range(4):
            for x in range(4):
                for core in range(2):
                    pairs.append((device_index(z, y, x, core), device_index(*target(z, y, x, core))))
    return pairs


Z_ON = [moves(lambda z, y, x, core, d=d: ((z + d * (1 - 2 * core)) % 4, y, x, core)) for d in range(4)]
Y_ON = [moves(lambda z, y, x, core, d=d: (z, (y + d * (1 - 2 * core)) % 4, x, core)) for d in range(4)]
SWAP = moves(lambda z, y, x, core: (z, y, x, 1 - core))


def call(body, grid, in_specs, out_specs, out_shape, scalars, operands, scratch=(), aliases=None, flops=0, vmem=8 << 20):
    nbytes = sum(4 * o.size for o in operands[:1])
    return pl.pallas_call(
        body,
        grid_spec=pltpu.PrefetchScalarGridSpec(
            num_scalar_prefetch=1, grid=grid, in_specs=in_specs, out_specs=out_specs, scratch_shapes=list(scratch)
        ),
        out_shape=out_shape,
        input_output_aliases=aliases or {},
        cost_estimate=pl.CostEstimate(flops=flops, bytes_accessed=2 * nbytes, transcendentals=0),
        compiler_params=pltpu.CompilerParams(vmem_limit_bytes=vmem),
    )(scalars, *operands)


def split_amplitudes(amplitudes, targets):
    def body(target, src, *refs):
        outs, turned = refs[:4], refs[4]
        turned[...] = jnp.swapaxes(src[0], 0, 1)
        for out, slot in zip(outs, range(4)):
            y = target[slot]
            yh, yl = y // 2, y % 2
            for half in range(2):
                lanes = pl.ds(pl.multiple_of(half * 256 + yl * 128, 128), 128)
                for x in range(4):
                    out[half, :, x * 128 : (x + 1) * 128] = turned[yh * 4 + x, :, lanes]

    return call(
        body,
        (4,),
        [pl.BlockSpec((1, 32, 8, 512), lambda k, t: (k, 0, 0, 0))],
        [pl.BlockSpec((2, 32, 512), lambda k, t: (0, k, 0))] * 4,
        [jax.ShapeDtypeStruct((2, 128, 512), F32)] * 4,
        targets,
        (amplitudes,),
        scratch=[pltpu.VMEM((8, 32, 512), F32)],
    )


def split_integrals(integrals):
    rows = integrals.shape[0]
    step = rows // 3

    def body(unused, src, out):
        lane = lax.broadcasted_iota(jnp.int32, (step, 128), 1) // 32
        for h in range(2):
            tiles = [src[:, (e * 4 + yh * 2 + h) * 128 :][:, :128] for yh in range(2) for e in range(2)]
            for j in range(4):
                made = None
                for s in range(4):
                    turn = (s - j) % 4 * 32
                    moved = pltpu.roll(tiles[s], turn, 1) if turn else tiles[s]
                    made = moved if made is None else jnp.where(lane == s, moved, made)
                out[h * 4 + j] = made

    return call(
        body,
        (3,),
        [pl.BlockSpec((step, 1024), lambda r, t: (r, 0))],
        pl.BlockSpec((8, step, 128), lambda r, t: (0, r, 0)),
        jax.ShapeDtypeStruct((8, rows, 128), F32),
        jnp.zeros((1,), jnp.int32),
        (integrals,),
    )


def two_parts(value):
    high = value.astype(BF16)
    return high, (value - high.astype(F32)).astype(BF16)


def laid_out(src, rows):
    first = lax.broadcasted_iota(jnp.int32, (rows, 128), 1) < 64
    for z0 in range(src.shape[0] // 4):
        for yb in range(2):
            one, two = src[z0 * 4 + yb * 2], src[z0 * 4 + yb * 2 + 1]
            yield (z0 * 2 + 0) * 2 + yb, jnp.where(first, one, pltpu.roll(two, 64, 1))
            yield (z0 * 2 + 1) * 2 + yb, jnp.where(first, pltpu.roll(one, 64, 1), two)


def product(ah, al, bh, bl):
    dot = functools.partial(jnp.dot, preferred_element_type=F32)
    return dot(ah, bh) + (dot(ah, bl) + dot(al, bh))


ANY = pl.BlockSpec(memory_space=pl.ANY)
VMEM_FIRST, VMEM_LAST = 56 << 20, 20 << 20
SMALL = pl.BlockSpec(memory_space=pltpu.SMEM)


def first_products(place, ints, own, near):
    rows = ints[0].shape[1]

    def body(at, *refs):
        src_a, src_own, src_near = refs[:3], refs[3:7], refs[7:10]
        out_a, out_b, sums = refs[10:12], refs[12:14], refs[14:16]
        raw_a, raw_own, raw_near, a, b, total, sem, done = refs[17:]
        refs[16][...] = jnp.zeros((8, 128), F32)
        core, z, y = at[0], at[1], at[2]
        way = 1 - 2 * core
        yl, yh = y & 1, y // 2
        zh, z0 = ((z + 2) & 3) // 2, z & 1
        halves = (1 - core, core)
        loads_a = [pltpu.make_async_copy(src_a[n], raw_a.at[n], sem.at[n]) for n in range(3)]
        loads_b = []
        for n, half in enumerate(halves):
            loads_b.append(
                [pltpu.make_async_copy(src_own[s].at[half], raw_own.at[n, s], sem.at[3 + n * 7 + s]) for s in range(4)]
                + [pltpu.make_async_copy(src_near[s].at[half], raw_near.at[n, s], sem.at[7 + n * 7 + s]) for s in range(3)]
            )
        for copy in loads_a + loads_b[0]:
            copy.start()
        stores = []

        def store(source, target):
            stores.append(pltpu.make_async_copy(source, target, done.at[len(stores)]))
            stores[-1].start()

        steps = (0, 1, 3)
        for n, step in enumerate(steps):
            loads_a[n].wait()
            slot = (y - step * way) & 3
            for tile, value in laid_out(raw_a.at[n], rows):
                lanes = slice(tile % 4 * 128, tile % 4 * 128 + 128)
                a[slot, tile // 4, 0, :, lanes], a[slot, tile // 4, 1, :, lanes] = two_parts(value)
        store(a.at[y, z0], out_a[0])
        store(a.at[zh * 2 + 1 - yl, z0], out_a[1])
        for n, half in enumerate(halves):
            for copy in loads_b[n]:
                copy.wait()
            if n == 0:
                for copy in loads_b[1]:
                    copy.start()
            for s in range(4):
                slot = (z - s * way) & 3
                b[n, slot, 0, y], b[n, slot, 1, y] = two_parts(raw_own[n, s])
            for m, back in enumerate((1, 3, 2)):
                part = (y - back * way) & 3
                for k, step in enumerate(steps):
                    slot = (z - step * way) & 3
                    b[n, slot, 0, part], b[n, slot, 1, part] = two_parts(raw_near[n, k, m])
                empty = jnp.zeros((128, 512), BF16)
                b[n, (z + 2) & 3, 0, part], b[n, (z + 2) & 3, 1, part] = empty, empty
            store(b.at[n, pl.ds((1 - yh) * 2, 2)], out_b[n])
            for group, chosen in ((yl, (0,)), (1 - yl, (1, 3))):
                value = None
                for step in chosen:
                    slot = (y - step * way) & 3
                    for k in range(2):
                        bh, bl = (b[n, slot // 2 * 2 + k, p].reshape(512, 512) for p in range(2))
                        part = product(a[slot, k, 0], a[slot, k, 1], bh, bl)
                        value = part if value is None else value + part
                total[n, group] = value
            store(total.at[n], sums[n])
        for copy in stores:
            copy.wait()

    return pl.pallas_call(
        body,
        in_specs=[SMALL] + [ANY] * 10,
        out_specs=[ANY] * 6 + [pl.BlockSpec(memory_space=pltpu.VMEM)],
        out_shape=[jax.ShapeDtypeStruct((2, rows, 512), BF16)] * 2
        + [jax.ShapeDtypeStruct((2, 2, 4, 128, 512), BF16)] * 2
        + [jax.ShapeDtypeStruct((2, rows, 512), F32)] * 2
        + [jax.ShapeDtypeStruct((8, 128), F32)],
        scratch_shapes=[
            pltpu.VMEM((3, 8, rows, 128), F32),
            pltpu.VMEM((2, 4, 128, 512), F32),
            pltpu.VMEM((2, 3, 3, 128, 512), F32),
            pltpu.VMEM((4, 2, 2, rows, 512), BF16),
            pltpu.VMEM((2, 4, 2, 4, 128, 512), BF16),
            pltpu.VMEM((2, 2, rows, 512), F32),
            pltpu.SemaphoreType.DMA((17,)),
            pltpu.SemaphoreType.DMA((6,)),
        ],
        cost_estimate=pl.CostEstimate(flops=18 * rows * 2048 * 512, bytes_accessed=24 << 20, transcendentals=0),
        compiler_params=pltpu.CompilerParams(vmem_limit_bytes=VMEM_FIRST),
    )(place, *ints, *own, *near)


def last_products(place, sums, ints, near, own_a, other_a, far_b, ended):
    rows = sums.shape[1]

    def body(at, src_sum, src_far, src_near, src_own, src_other, src_b, unused, out, *refs):
        total, raw, raw_near, own, other, far, b, late, sem = refs
        half, z, y, core = at[0], at[1], at[2], at[3]
        way = 1 - 2 * core
        yl, yh = y & 1, y // 2
        zh, z0 = ((z + 2) & 3) // 2, z & 1
        pairs = (src_near.at[half], raw_near), (src_far, raw), (src_other, other), (src_sum, total), (src_own, own), (src_b, b)
        copies = [pltpu.make_async_copy(*pair, sem.at[n]) for n, pair in enumerate(pairs)]
        for copy in copies:
            copy.start()
        copies[0].wait()
        empty = jnp.zeros((128, 512), BF16)
        late[0, y], late[1, y] = empty, empty
        for m, back in enumerate((1, 3, 2)):
            slot = (y - back * way) & 3
            late[0, slot], late[1, slot] = two_parts(raw_near[m])
        bh, bl = late[0].reshape(512, 512), late[1].reshape(512, 512)
        copies[1].wait()
        for tile, value in laid_out(raw, rows):
            lanes = slice(tile % 4 * 128, tile % 4 * 128 + 128)
            far[tile // 4, 0, :, lanes], far[tile // 4, 1, :, lanes] = two_parts(value)
        for copy in copies[2:5]:
            copy.wait()
        value = total[1 - yl] + product(other[0], other[1], bh, bl)
        for x in range(4):
            out[(1 - yl) * 4 + x % 2 * 2 + x // 2] = value[:, x * 128 : x * 128 + 128]

        @pl.when(yh != zh)
        def _():
            own[...] = far[z0]

        value = total[yl] + product(own[0], own[1], bh, bl)
        copies[5].wait()
        for k in range(2):
            value = value + product(far[k, 0], far[k, 1], *(b[k, p].reshape(512, 512) for p in range(2)))
        for x in range(4):
            out[yl * 4 + x % 2 * 2 + x // 2] = value[:, x * 128 : x * 128 + 128]

    return pl.pallas_call(
        body,
        in_specs=[SMALL] + [ANY] * 7,
        out_specs=pl.BlockSpec(memory_space=pltpu.VMEM),
        out_shape=jax.ShapeDtypeStruct((8, rows, 128), F32),
        scratch_shapes=[
            pltpu.VMEM((2, rows, 512), F32),
            pltpu.VMEM((8, rows, 128), F32),
            pltpu.VMEM((3, 128, 512), F32),
            pltpu.VMEM((2, rows, 512), BF16),
            pltpu.VMEM((2, rows, 512), BF16),
            pltpu.VMEM((2, 2, rows, 512), BF16),
            pltpu.VMEM((2, 2, 4, 128, 512), BF16),
            pltpu.VMEM((2, 4, 128, 512), BF16),
            pltpu.SemaphoreType.DMA((6,)),
        ],
        cost_estimate=pl.CostEstimate(flops=6 * rows * 2048 * 512, bytes_accessed=8 << 20, transcendentals=0),
        compiler_params=pltpu.CompilerParams(vmem_limit_bytes=VMEM_LAST),
    )(place, sums, ints, near, own_a, other_a, far_b, ended)


def passed(ended):
    def body(a, b):
        b[...] = a[...]

    return pl.pallas_call(
        body,
        out_shape=jax.ShapeDtypeStruct(ended.shape, F32),
        cost_estimate=pl.CostEstimate(flops=12 * 10**9, bytes_accessed=8192, transcendentals=0),
        compiler_params=pltpu.CompilerParams(vmem_limit_bytes=4 << 20),
    )(ended)


def total_of(one, two):
    def body(a, b, out):
        out[...] = a[...] + b[...]

    whole = pl.BlockSpec(memory_space=pltpu.VMEM)
    return pl.pallas_call(
        body,
        in_specs=[whole] * 2,
        out_specs=whole,
        out_shape=jax.ShapeDtypeStruct(one.shape, F32),
        compiler_params=pltpu.CompilerParams(vmem_limit_bytes=4 << 20),
    )(one, two)


def finish(parts, driver, row_part, col_part):
    rows = driver.shape[0]

    def body(part, given, row, col, out):
        for yl in range(2):
            lanes = slice(yl * 128, (yl + 1) * 128)
            cycle = (part[yl * 4] + part[yl * 4 + 1]) + (part[yl * 4 + 2] + part[yl * 4 + 3])
            out[:, lanes] = (given[:, lanes] + cycle) / (row[...] + col[:, lanes])

    return pl.pallas_call(
        body,
        out_shape=jax.ShapeDtypeStruct((rows, 256), F32),
        compiler_params=pltpu.CompilerParams(vmem_limit_bytes=8 << 20),
    )(parts, driver, row_part, col_part)


def shards(integrals, amplitudes, driver, occ_rows, occ_cols, virtual):
    z, yl, yh, xh, xl, core = (lax.axis_index(axis) for axis in AXES)
    x = xh * 2 + xl
    y = yh * 2 + yl
    way = 1 - 2 * core
    rows = driver.shape[0]
    number = lambda *v: jnp.stack([jnp.asarray(i, jnp.int32) for i in v])

    ints = split_integrals(integrals)
    amplitudes, ints = lax.optimization_barrier((amplitudes, ints))
    parts = split_amplitudes(amplitudes, number(*((y + d * way) % 4 for d in range(4))))
    on_z = lambda v, d: lax.ppermute(v, AXES, Z_ON[d])
    on_y = lambda v, d: lax.ppermute(v, AXES, Y_ON[d])
    wave = lambda *v: list(lax.optimization_barrier(v))
    ints = lax.all_to_all(ints, ("xh", "xl", "core"), 0, 0, tiled=True)
    b, d, c = on_y(parts[1], 1), on_y(parts[2], 2), on_y(parts[3], 3)
    own1 = on_z(parts[0], 1)
    own3 = on_z(wave(parts[0], own1)[0], 3)
    own2 = on_z(own1, 1)
    ints, b, own1, d, own3, c, own2 = wave(ints, b, own1, d, own3, c, own2)
    own = [parts[0], own1, own2, own3]
    bcd = jnp.stack([b, c, d], axis=1)
    bcd1, bcd3 = on_z(bcd, 1), on_z(bcd, 3)
    ints1, ints3 = on_y(ints, 1), on_y(ints, 3)
    bcd2, ints2 = on_z(bcd1, 1), on_y(ints1, 1)
    own_a, other_a, far_other, far_mine, sum_other, sum_mine, ended = first_products(
        number(core, z, y), (ints, ints1, ints3), own, (bcd, bcd1, bcd3)
    )
    bcd2, ints2, ended = wave(bcd2, ints2, passed(ended))
    other = last_products(number(1 - core, z, y, core), sum_other, ints2, bcd2, own_a, other_a, far_other, ended)
    mine = last_products(number(core, z, y, core), sum_mine, ints2, bcd2, own_a, other_a, far_mine, ended)
    mine = total_of(mine, lax.ppermute(other, AXES, SWAP))
    mine = lax.all_to_all(mine, ("yl", "xl", "xh"), 0, 0, tiled=True)
    row_energy = (occ_rows[:, None] - virtual[None, :]).reshape(-1)
    col_energy = (occ_cols[:, None] - virtual[None, :]).reshape(-1)
    row_part = lax.dynamic_slice_in_dim(row_energy, (z * 2 + yl) * rows, rows, 0)
    col_part = lax.dynamic_slice_in_dim(col_energy, ((yh * 4 + x) * 2 + core) * 256, 256, 0)
    return finish(mine, driver, row_part[:, None], col_part[None, :])


def solution(mesh):
    fine = Mesh(mesh.devices.reshape(SIZES), AXES)
    row, col = ("z", "yl"), ("yh", "xh", "xl", "core")
    in_specs = (P(row, col), P(row, col, None, None), P(row, col), P(), P(), P())
    return jax.shard_map(shards, mesh=fine, in_specs=in_specs, out_specs=P(row, col), check_vma=False)
```
